32 devices in a mesh: groups: 2 (over x), store: 8 (over z, y), head: 2 (over core).
Axes of the slice: x: 2, y: 2, z: 4, core: 2. Of those that a mesh axis runs over, the one named last changes fastest.
Arguments:
- tokens_in: bfloat16 [16384, 2048], P(('groups', 'store', 'head')), parts along dimension 0, may hold values from -6 to 6
- w_query: bfloat16 [2048, 1024], P(None, 'head'), may hold values from -0.125 to 0.125
- w_key: bfloat16 [2048, 1024], P(None, 'head'), may hold values from -0.125 to 0.125
- w_value: bfloat16 [2048, 2048], P(None, 'head'), may hold values from -0.125 to 0.125
- w_zgate: bfloat16 [2048, 2048], P(None, 'head'), may hold values from -0.125 to 0.125
- w_gates: bfloat16 [2, 2048, 16], P(None, None, 'head'), may hold values from -0.125 to 0.125
- w_out: bfloat16 [2048, 2048], P('head'), may hold values from -0.125 to 0.125
- decay_log: float32 [16], P('head'), may hold values from -8.5 to -2.5
- dt_bias: float32 [16], P('head'), may hold values from -2 to 2
- norm_gain: float32 [128], replicated, may hold values from 0.1 to 1.9
- init_state: float32 [16, 128, 128], P('head'), may hold values from -8 to 8
- doc_trans: bfloat16 [64, 16, 128, 128], P(('groups', 'store'), 'head'), parts along dimension 0, may hold values from -0.15 to 1
- doc_state: bfloat16 [64, 16, 128, 128], P(('groups', 'store'), 'head'), parts along dimension 0, may hold values from -1.1953125 to 1.1953125
- retrieval: int32 [16, 16], P('groups'), parts along dimension 0, may hold values from 0 to 31, as said below
- doc_place: int32 [64], P('groups'), parts along dimension 0, may hold values from 0 to 31, as said below
- assignment: int32 [16], P('groups'), parts along dimension 0, may hold values from 0 to 7, each once
Outputs:
- layer_out: bfloat16 [16384, 2048], P(('groups', 'store', 'head')), parts along dimension 0
The draws below stay inside these ranges and needn't reach their ends.
There are 2 independent parts, one for each index of `groups`. The reference program is written for one: setup_inputs(seed, part) draws one part's arguments, and reference() takes and returns one part's arrays. A program takes and returns all parts, laid end to end along the dimension named above; an argument that names none is the same for every part. Nothing has to cross between parts.
Inputs may be any that keep to these rules, and one draw needn't show every extreme that they name: `retrieval`: each row names 16 different documents; in every row at most 2 of them have doc_place in the 4 rows of one store device (equal doc_place // 4), and exactly 2 for at least one device. A permutation: document d lies in row doc_place[d] of doc_trans and doc_state.
All inputs are finite; a program needn't handle non-finite values.
Results may differ from the reference program's by a relative error of at most 0.011.
Values may be sent and summed in bfloat16 or wider, within the bound.
A program may use at most 192 MiB of HBM per device.

```python
import jax
import jax.numpy as jnp
from jax import lax

D = 2048
HK = 8
HV = 16
DK = 128
DV = 128
SPAN = 64
LIST = 16
CAP = 2
DOC_DEV = 4
TOK = 1024
REQ = 8
DOCS = 32
TOKENS = 8192
N_STORE = 8


def store_layout(key):
    key_place = jax.random.fold_in(key, 101)
    key_forced = jax.random.fold_in(key, 102)
    key_owner = jax.random.fold_in(key, 103)
    key_popular = jax.random.fold_in(key, 104)
    key_pick = jax.random.fold_in(key, 105)
    key_order = jax.random.fold_in(key, 106)
    placement = jax.random.permutation(key_place, DOCS).astype(jnp.int32)
    holder = jnp.argsort(placement).astype(jnp.int32)
    slot_total = N_STORE * CAP
    slot_ids = jnp.arange(slot_total, dtype=jnp.int32)
    item_owner = slot_ids // CAP
    forced = jax.random.randint(key_forced, (REQ, 1), 0, N_STORE, dtype=jnp.int32)
    scores = jax.random.randint(key_owner, (REQ, slot_total), 0, 1 << 20, dtype=jnp.int32) * slot_total + slot_ids[None, :]
    scores = jnp.where(item_owner[None, :] == forced, -1 - slot_ids[None, :], scores)
    chosen = jnp.argsort(scores, axis=1)[:, :LIST].astype(jnp.int32)
    owner_of = chosen // CAP
    copy_of = chosen % CAP
    levels = jax.random.randint(key_popular, (DOCS,), 0, 5, dtype=jnp.int32)
    popularity = jnp.left_shift(jnp.ones_like(levels), levels)
    pick_scores = jax.random.randint(key_pick, (REQ, N_STORE, DOC_DEV), 0, 1 << 16, dtype=jnp.int32) // popularity.reshape(N_STORE, DOC_DEV)[None]
    pick_scores = pick_scores * DOC_DEV + jnp.arange(DOC_DEV, dtype=jnp.int32)
    local_order = jnp.argsort(pick_scores, axis=2).astype(jnp.int32).reshape(REQ, N_STORE * DOC_DEV)
    local_rows = jnp.take_along_axis(local_order, owner_of * DOC_DEV + copy_of, axis=1)
    store_rows = owner_of * DOC_DEV + local_rows
    order_scores = jax.random.randint(key_order, (REQ, LIST), 0, 1 << 20, dtype=jnp.int32) * LIST + jnp.arange(LIST, dtype=jnp.int32)
    shuffle = jnp.argsort(order_scores, axis=1).astype(jnp.int32)
    store_rows = jnp.take_along_axis(store_rows, shuffle, axis=1)
    return (placement, holder[store_rows].astype(jnp.int32))


def draw_retrieval(key, part):
    layout = store_layout(key)
    return layout[1]


def draw_doc_place(key, part):
    layout = store_layout(key)
    return layout[0]


def draw_decay_log(key, part):
    key = jax.random.fold_in(key, 5)
    rates = jax.random.uniform(key, (HV,), jnp.float32, -6.8, -2.5)
    return rates


def draw_doc_trans(key, part):
    key = jax.random.fold_in(key, 3)
    key_diag = jax.random.fold_in(key, 1)
    key_off = jax.random.fold_in(key, 2)
    shape = (DOCS, HV, DK, DK)
    spread = 0.2 * DK ** (-0.5)
    diagonal = jax.random.uniform(key_diag, (DOCS, HV, DK), jnp.float32, 0.85, 1.0)
    coupling = jnp.clip(spread * jax.random.normal(key_off, shape, jnp.float32), -4.0 * spread, 4.0 * spread)
    on_diagonal = jnp.arange(DK)[:, None] == jnp.arange(DK)[None, :]
    return jnp.where(on_diagonal, diagonal[..., :, None], coupling).astype(jnp.bfloat16)


def block_scale(rng, dims, pieces, low, high):
    level, own = 1.0, jax.random.fold_in(rng, 6)
    for axis_at, shards_of in pieces:
        draws = jnp.exp(jax.random.uniform(jax.random.fold_in(own, axis_at), (shards_of,), jnp.float32, low / len(pieces), high / len(pieces)))
        level = level * jnp.repeat(draws, dims[axis_at] // shards_of).reshape([-1 if axis == axis_at else 1 for axis in range(len(dims))])
    return level


def scatter_about(own_key, shape, scale, bound, pieces=(), kind=jnp.bfloat16):
    gain = block_scale(own_key, shape, pieces, -0.22, 0.18) if pieces else 1.0
    entries = jax.random.normal(own_key, shape, jnp.float32) * scale * gain
    return jnp.minimum(jnp.maximum(entries, -bound), bound).astype(kind)


def setup_inputs(seed: int = 0, part: int = 0) -> dict:
    key_of = jax.random.split(jax.random.key(seed), 17)
    part_keys = jax.random.split(jax.random.fold_in(key_of[16], part), 17)
    tokens_in = scatter_about(part_keys[0], (TOKENS, D), 1.0, 6.0, ((0, 16),))
    w_query = scatter_about(key_of[1], (D, HK * DK), D ** -0.5, 0.125, ((1, 2),))
    w_key = scatter_about(key_of[2], (D, HK * DK), D ** -0.5, 0.125, ((1, 2),))
    w_value = scatter_about(key_of[3], (D, HV * DV), D ** -0.5, 0.125, ((1, 2),))
    w_zgate = scatter_about(key_of[4], (D, HV * DV), D ** -0.5, 0.125, ((1, 2),))
    w_gates = scatter_about(key_of[5], (2, D, HV), D ** -0.5, 0.125, ((2, 2),))
    w_out = scatter_about(key_of[6], (HV * DV, D), (HV * DV) ** -0.5, 0.125, ((0, 2),))
    decay_log = draw_decay_log(jax.random.fold_in(key_of[16], 71), part)
    dt_bias = jnp.clip(jax.random.uniform(key_of[8], (HV,), jnp.float32, -2.0, 2.0) * block_scale(key_of[8], (HV,), ((0, 2),), -0.4, 0.0), -2.0, 2.0)
    norm_gain = jnp.clip(1.0 + 0.18 * jax.random.normal(key_of[9], (DV,), jnp.float32), 0.1, 1.9)
    init_state = scatter_about(key_of[10], (HV, DK, DV), 2.0, 8.0, ((0, 2),), jnp.float32)
    doc_trans = draw_doc_trans(jax.random.fold_in(jax.random.fold_in(key_of[16], part), 71), part)
    doc_state = scatter_about(part_keys[12], (DOCS, HV, DK, DV), 0.2, 1.1953125, ((0, 8), (1, 2)))
    retrieval = draw_retrieval(jax.random.fold_in(jax.random.fold_in(key_of[16], part), 71), part)
    doc_place = draw_doc_place(jax.random.fold_in(jax.random.fold_in(key_of[16], part), 71), part)
    assignment = jax.random.permutation(part_keys[15], REQ).astype(jnp.int32)
    return dict(tokens_in=tokens_in, w_query=w_query, w_key=w_key, w_value=w_value, w_zgate=w_zgate, w_gates=w_gates, w_out=w_out, decay_log=decay_log, dt_bias=dt_bias, norm_gain=norm_gain, init_state=init_state, doc_trans=doc_trans, doc_state=doc_state, retrieval=retrieval, doc_place=doc_place, assignment=assignment)


highest = lax.Precision.HIGHEST

def contract(form, left, right):
    return jnp.einsum(form, left, right, precision=highest)

def unit_lower_inverse(strict_part):
    on_diagonal = jnp.eye(strict_part.shape[-1], dtype=strict_part.dtype)
    powered = -strict_part
    inverse = on_diagonal + powered
    for doubling in range(strict_part.shape[-1].bit_length() - 2):
        powered = contract('...ij,...jk->...ik', powered, powered)
        inverse = inverse + contract('...ij,...jk->...ik', inverse, powered)
    return inverse

def normalize_rows(values, factor):
    return values * lax.rsqrt(lax.optimization_barrier(jnp.sum(values * values, axis=-1, keepdims=True)) + 1e-06) * factor

def span_terms(queries, keys_all, values, beta_rows, logdecay):
    queries = queries.astype(jnp.float32)
    keys_all = keys_all.astype(jnp.float32)
    values = values.astype(jnp.float32)
    positions = jnp.arange(SPAN)
    strict = positions[:, None] > positions[None, :]
    lower_mask = positions[:, None] >= positions[None, :]
    cumulative = jnp.cumsum(logdecay, axis=-1)
    spread = cumulative[..., :, None] - cumulative[..., None, :]
    pair_decay = jnp.exp(jnp.where(lower_mask, spread, 0.0))
    key_key = contract('hncd,hnmd->hncm', keys_all, keys_all)
    query_key = contract('hncd,hnmd->hncm', queries, keys_all)
    lower_mix = jnp.where(strict, pair_decay * key_key * beta_rows[..., None, :], 0.0)
    attend = jnp.where(lower_mask, pair_decay * query_key * beta_rows[..., None, :], 0.0)
    growth = jnp.exp(cumulative)
    inverse = unit_lower_inverse(lower_mix)
    corrected = contract('hncm,hnmv->hncv', inverse, values)
    weighted = contract('hncm,hnmd->hncd', inverse, growth[..., None] * keys_all)
    tail_weight = jnp.exp(cumulative[..., -1:] - cumulative) * beta_rows
    return (growth[..., None] * queries, attend, corrected, weighted, tail_weight[..., None] * keys_all, growth[..., -1])

def span_step(carried, block_terms):
    scaled_query, attend, corrected, weighted, tail_keys, closing = block_terms
    correction = corrected - contract('hcd,hdv->hcv', weighted, carried)
    output = contract('hcd,hdv->hcv', scaled_query, carried) + contract('hcm,hmv->hcv', attend, correction)
    carried = closing[:, None, None] * carried + contract('hcd,hcv->hdv', tail_keys, correction)
    return (carried, output)

def prepare(proj_query, proj_key, proj_value, pre_decay, pre_beta, decay_log, dt_bias):
    tokens = proj_query.shape[0]
    heads_v = decay_log.shape[0]
    heads_k = proj_query.shape[1] // DK
    group_size = heads_v // heads_k
    queries = normalize_rows(proj_query.astype(jnp.float32).reshape(tokens, heads_k, DK), DK ** (-0.5)).astype(jnp.bfloat16)
    keys_all = normalize_rows(proj_key.astype(jnp.float32).reshape(tokens, heads_k, DK), 1.0).astype(jnp.bfloat16)
    queries = jnp.repeat(queries, group_size, axis=1)
    keys_all = jnp.repeat(keys_all, group_size, axis=1)
    values = proj_value.reshape(tokens, heads_v, DV)
    beta_rows = jax.nn.sigmoid(pre_beta.astype(jnp.float32))
    logdecay = -jnp.exp(decay_log) * jax.nn.softplus(pre_decay.astype(jnp.float32) + dt_bias)
    blocks = tokens // SPAN

    def heads_first(tensor):
        swapped = jnp.moveaxis(tensor, 1, 0)
        return swapped.reshape((heads_v, blocks, SPAN) + swapped.shape[2:])
    return span_terms(heads_first(queries), heads_first(keys_all), heads_first(values), heads_first(beta_rows), heads_first(logdecay))

def compose(init_state, fetched_trans, fetched_state):

    def advance(carried, doc_pair):
        updated = contract('hij,hjv->hiv', doc_pair[0].astype(jnp.float32), carried) + doc_pair[1].astype(jnp.float32)
        return (updated, None)
    return lax.scan(advance, init_state, (fetched_trans, fetched_state))[0]

def gated_mix(outputs, proj_gate, norm_gain):
    blocks, heads_v, block_len, feature_width = outputs.shape
    core_out = jnp.moveaxis(outputs, 1, 0).reshape(heads_v, blocks * block_len, feature_width)
    core_out = jnp.moveaxis(core_out, 0, 1)
    gate_values = proj_gate.astype(jnp.float32).reshape(core_out.shape)
    normed = core_out * lax.rsqrt(lax.optimization_barrier(jnp.mean(core_out * core_out, axis=-1, keepdims=True)) + 1e-06) * norm_gain * jax.nn.silu(gate_values)
    return normed.reshape(core_out.shape[0], heads_v * feature_width).astype(jnp.bfloat16)

def reference(tokens_in, w_query, w_key, w_value, w_zgate, w_gates, w_out, decay_log, dt_bias, norm_gain, init_state, doc_trans, doc_state, retrieval, doc_place, assignment):

    def one_request(inputs):
        token_rows, slot_index = inputs
        request = assignment[slot_index]
        store_rows = doc_place[retrieval[request]]
        start_state = compose(init_state, doc_trans[store_rows], doc_state[store_rows])
        proj_query = jnp.dot(token_rows, w_query, preferred_element_type=jnp.float32).astype(jnp.bfloat16)
        proj_key = jnp.dot(token_rows, w_key, preferred_element_type=jnp.float32).astype(jnp.bfloat16)
        proj_value = jnp.dot(token_rows, w_value, preferred_element_type=jnp.float32).astype(jnp.bfloat16)
        proj_gate = jnp.dot(token_rows, w_zgate, preferred_element_type=jnp.float32).astype(jnp.bfloat16)
        pre_decay = jnp.dot(token_rows, w_gates[0], preferred_element_type=jnp.float32).astype(jnp.bfloat16)
        pre_beta = jnp.dot(token_rows, w_gates[1], preferred_element_type=jnp.float32).astype(jnp.bfloat16)
        block_terms = prepare(proj_query, proj_key, proj_value, pre_decay, pre_beta, decay_log, dt_bias)
        by_block = tuple((jnp.moveaxis(tensor, 1, 0) for tensor in block_terms))
        outputs = lax.scan(span_step, start_state, by_block)[1]
        mixed_rows = gated_mix(outputs, proj_gate, norm_gain)
        return jnp.dot(mixed_rows, w_out, preferred_element_type=jnp.float32).astype(jnp.bfloat16)
    token_blocks = tokens_in.reshape(REQ, TOK, tokens_in.shape[1])
    results = lax.map(one_request, (token_blocks, jnp.arange(REQ, dtype=jnp.int32)))
    return results.reshape(REQ * TOK, tokens_in.shape[1])
```

```python
import jax
import jax.numpy as jnp
from jax import lax
from jax.experimental import pallas as pl
from jax.experimental.pallas import tpu as pltpu
from jax.sharding import PartitionSpec as P

DK = 128
DV = 128
CHUNK = 128
ROWS = 256
BF = jnp.bfloat16
F32 = jnp.float32


def mm(left, right):
    return jnp.dot(left, right, preferred_element_type=F32)


def unit_lower_inverses(mixes):
    size = mixes[0].shape[0]
    row = lax.broadcasted_iota(jnp.int32, (size, size), 0)
    col = lax.broadcasted_iota(jnp.int32, (size, size), 1)
    eye = jnp.where(row == col, 1.0, 0.0)
    inside = row // 16 == col // 16
    powers = [jnp.where(inside, -mix, 0.0) for mix in mixes]
    inverses = [eye + power for power in powers]
    powers = [mm(power.astype(BF), power.astype(BF)) for power in powers]
    for last in (False, False, True):
        if last:
            products = [mm(x.astype(BF), p.astype(BF)) for x, p in zip(inverses, powers)]
            inverses = [x + y for x, y in zip(inverses, products)]
        else:
            products = [
                mm(jnp.concatenate([x.astype(BF), p.astype(BF)], axis=0), p.astype(BF))
                for x, p in zip(inverses, powers)
            ]
            inverses = [x + y[:size] for x, y in zip(inverses, products)]
            powers = [y[size:] for y in products]
    width = 16
    while width < size:
        between = (row // (2 * width) == col // (2 * width)) & (row // width != col // width)
        narrow = [x.astype(BF) for x in inverses]
        steps = [mm(jnp.where(between, mix, 0.0).astype(BF), x) for mix, x in zip(mixes, narrow)]
        steps = [mm(x, step.astype(BF)) for x, step in zip(narrow, steps)]
        inverses = [x - step for x, step in zip(inverses, steps)]
        width *= 2
    return inverses


def delta_kernel(
    closing, x, w_q, w_k, w_v, w_z, cols, rows, gate, core, linear, q_s, k_s, v_s, qw_s, at_s, u_s, state
):
    step = pl.program_id(0)
    steps = pl.num_programs(0)
    tokens = x.shape[0]
    chunks = tokens // CHUNK
    heads = core.shape[1] // DV

    @pl.loop(0, tokens // ROWS)
    def project(tile):
        at = pl.ds(pl.multiple_of(tile * ROWS, ROWS), ROWS)
        part = x[at, :]
        q = mm(part, w_q[...]).astype(BF).astype(F32)
        q_s[at, :] = (
            q * lax.rsqrt(jnp.sum(q * q, axis=-1, keepdims=True) + 1e-06) * DK ** (-0.5)
        ).astype(BF)
        k = mm(part, w_k[...]).astype(BF).astype(F32)
        k_s[at, :] = (k * lax.rsqrt(jnp.sum(k * k, axis=-1, keepdims=True) + 1e-06)).astype(BF)
        v_s[at, :] = mm(part, w_v[...]).astype(BF)
        gate[at, :] = mm(part, w_z[...]).astype(BF)

    group = min(4, chunks)

    @pl.loop(0, chunks // group)
    def terms(quarter):
        row = lax.broadcasted_iota(jnp.int32, (CHUNK, CHUNK), 0)
        col = lax.broadcasted_iota(jnp.int32, (CHUNK, CHUNK), 1)
        kept, mixes = [], []
        for inner in range(group):
            chunk = quarter * group + inner
            at = pl.ds(pl.multiple_of(chunk * CHUNK, CHUNK), CHUNK)
            q, k, v = q_s[at, :], k_s[at, :], v_s[at, :]
            both = lax.dot_general(
                jnp.concatenate([k, q], axis=0), k, (((1,), (1,)), ((), ())), preferred_element_type=F32
            )
            k_wide = k.astype(F32)
            k_turned = k_wide.T
            for e in range(2):
                cum_c = cols[0, at, e : e + 1]
                cum_r = rows[0, e : e + 1, at]
                beta_r = rows[0, 2 + e : 3 + e, at]
                decay = jnp.exp(jnp.where(row >= col, cum_c - cum_r, 0.0)) * beta_r
                mixes.append(jnp.where(row > col, decay * both[:CHUNK], 0.0))
                attend = jnp.where(row >= col, decay * both[CHUNK:], 0.0)
                growth = jnp.exp(cum_c)
                tail = jnp.exp(cum_r[:, CHUNK - 1 :] - cum_r) * beta_r
                head = 2 * step + e
                at_s[head, chunk] = jnp.concatenate([attend, k_turned * tail], axis=0).astype(BF)
                qw_s[head, chunk, :CHUNK, :] = (growth * q.astype(F32)).astype(BF)
                side = jnp.concatenate(
                    [v[:, e * DV : (e + 1) * DV], (growth * k_wide).astype(BF)], axis=1
                )
                kept.append((head, chunk, side))
        for inverse, (head, chunk, side) in zip(unit_lower_inverses(mixes), kept):
            solved = mm(inverse.astype(BF), side)
            u_s[head, chunk] = solved[:, :DV]
            qw_s[head, chunk, CHUNK:, :] = solved[:, DV:].astype(BF)

    @pl.when(step == steps - 1)
    def scan():
        row = lax.broadcasted_iota(jnp.int32, (DK, DV + DK), 0)
        col = lax.broadcasted_iota(jnp.int32, (DK, DV + DK), 1)
        start = jnp.where(row + DV == col, 1.0, 0.0)
        for head in range(heads):
            state[head] = start

        @pl.loop(0, chunks)
        def advance(chunk):
            at = pl.ds(pl.multiple_of(chunk * CHUNK, CHUNK), CHUNK)
            firsts = [mm(qw_s[head, chunk], state[head].astype(BF)) for head in range(heads)]
            seconds = []
            for head, first in enumerate(firsts):
                lower = first[CHUNK:]
                u = jnp.concatenate([u_s[head, chunk] - lower[:, :DV], -lower[:, DV:]], axis=1)
                seconds.append(mm(at_s[head, chunk], u.astype(BF)))
            for head, (first, second) in enumerate(zip(firsts, seconds)):
                out = first[:CHUNK] + second[:CHUNK]
                core[at, head * DV : (head + 1) * DV] = out[:, :DV]
                linear[at, head * DK : (head + 1) * DK] = out[:, DV:].astype(BF)
                state[head] = closing[head, chunk] * state[head] + second[CHUNK:]


def delta_terms(x, w_query, w_key, w_value, w_zgate, cumulative, beta):
    tokens, width = x.shape
    heads = beta.shape[0]
    steps = heads // 2
    chunks = tokens // CHUNK
    closing = jnp.exp(cumulative[:, CHUNK - 1 :: CHUNK])
    rows = jnp.concatenate([cumulative.reshape(steps, 2, tokens), beta.reshape(steps, 2, tokens)], axis=1)
    cols = jnp.swapaxes(rows, 1, 2)
    flops = 2 * tokens * width * 6 * DK * steps + heads * chunks * 26 * 2 * 128**3
    return pl.pallas_call(
        delta_kernel,
        grid=(steps,),
        in_specs=[
            pl.BlockSpec(memory_space=pltpu.SMEM),
            pl.BlockSpec((tokens, width), lambda i: (0, 0)),
            pl.BlockSpec((width, DK), lambda i: (0, i)),
            pl.BlockSpec((width, DK), lambda i: (0, i)),
            pl.BlockSpec((width, 2 * DV), lambda i: (0, i)),
            pl.BlockSpec((width, 2 * DV), lambda i: (0, i)),
            pl.BlockSpec((1, tokens, 4), lambda i: (i, 0, 0)),
            pl.BlockSpec((1, 4, tokens), lambda i: (i, 0, 0)),
        ],
        out_specs=[
            pl.BlockSpec((tokens, 2 * DV), lambda i: (0, i)),
            pl.BlockSpec((tokens, heads * DV), lambda i: (0, 0)),
            pl.BlockSpec((tokens, heads * DK), lambda i: (0, 0)),
        ],
        out_shape=[
            jax.ShapeDtypeStruct((tokens, heads * DV), BF),
            jax.ShapeDtypeStruct((tokens, heads * DV), F32),
            jax.ShapeDtypeStruct((tokens, heads * DK), BF),
        ],
        scratch_shapes=[
            pltpu.VMEM((tokens, DK), BF),
            pltpu.VMEM((tokens, DK), BF),
            pltpu.VMEM((tokens, 2 * DV), BF),
            pltpu.VMEM((heads, chunks, 2 * CHUNK, DK), BF),
            pltpu.VMEM((heads, chunks, CHUNK + DK, CHUNK), BF),
            pltpu.VMEM((heads, chunks, CHUNK, DV), F32),
            pltpu.VMEM((heads, DK, DV + DK), F32),
        ],
        compiler_params=pltpu.CompilerParams(
            dimension_semantics=("arbitrary",), vmem_limit_bytes=56 * 2**20
        ),
        cost_estimate=pl.CostEstimate(flops=flops * 3, bytes_accessed=28 * 2**20, transcendentals=0),
    )(closing, x, w_query, w_key, w_value, w_zgate, cols, rows)


def compose_kernel(order, init, docs, out):
    slots, listed = order.shape

    def advance(j, carry):
        for slot in range(slots):
            doc = order[slot, j]
            state = out[slot]
            high = state.astype(BF)
            low = (state - high.astype(F32)).astype(BF)
            moved = mm(docs[doc, :DK, :], jnp.concatenate([high, low], axis=1))
            out[slot] = moved[:, :DV] + moved[:, DV:] + docs[doc, DK:, :].astype(F32)
        return carry

    for slot in range(slots):
        out[slot] = init[...]
    lax.fori_loop(0, listed, advance, 0)


def compose(order, init, docs):
    slots, listed = order.shape
    return pl.pallas_call(
        compose_kernel,
        in_specs=[
            pl.BlockSpec(memory_space=pltpu.SMEM),
            pl.BlockSpec(memory_space=pltpu.VMEM),
            pl.BlockSpec(memory_space=pltpu.VMEM),
        ],
        out_specs=pl.BlockSpec(memory_space=pltpu.VMEM),
        out_shape=jax.ShapeDtypeStruct((slots, DK, DV), F32),
        compiler_params=pltpu.CompilerParams(vmem_limit_bytes=24 * 2**20),
        cost_estimate=pl.CostEstimate(
            flops=slots * listed * 4 * 128**3 * 8, bytes_accessed=4 * 2**20, transcendentals=0
        ),
    )(order, init, docs)


def gate_kernel(half, core, linear, gate, start, gain, out):
    del half
    for head in range(start.shape[0]):
        at = slice(head * DV, (head + 1) * DV)
        state = start[head]
        high = state.astype(BF)
        low = (state - high.astype(F32)).astype(BF)
        moved = mm(linear[:, at], jnp.concatenate([high, low], axis=1))
        values = core[:, at] + moved[:, :DV] + moved[:, DV:]
        z = gate[:, at].astype(F32)
        mean = jnp.mean(values * values, axis=-1, keepdims=True)
        out[:, at] = (values * lax.rsqrt(mean + 1e-06) * gain[...] * (z * jax.nn.sigmoid(z))).astype(BF)


def gated(half, core, linear, gate, start, gain):
    tokens, width = core.shape
    tiles = tokens // 2 // ROWS
    block = pl.BlockSpec((ROWS, width), lambda i, half: (half[0] * tiles + i, 0))
    return pl.pallas_call(
        gate_kernel,
        grid_spec=pltpu.PrefetchScalarGridSpec(
            num_scalar_prefetch=1,
            grid=(tiles,),
            in_specs=[
                block,
                block,
                block,
                pl.BlockSpec(start.shape, lambda i, half: (0, 0, 0)),
                pl.BlockSpec((1, DV), lambda i, half: (0, 0)),
            ],
            out_specs=pl.BlockSpec((ROWS, width), lambda i, half: (i, 0)),
        ),
        out_shape=jax.ShapeDtypeStruct((tokens // 2, width), BF),
        compiler_params=pltpu.CompilerParams(
            dimension_semantics=("arbitrary",), vmem_limit_bytes=24 * 2**20
        ),
        cost_estimate=pl.CostEstimate(flops=2**30, bytes_accessed=5 * 2**20, transcendentals=0),
    )(half, core, linear, gate, start, gain)


def decays(x, w_gates, decay_log, dt_bias):
    heads = decay_log.shape[0]
    weights = jnp.concatenate([w_gates[0], w_gates[1]], axis=1)
    pre = lax.dot_general(weights, x, (((0,), (1,)), ((), ())), preferred_element_type=F32)
    pre = pre.astype(BF).astype(F32)
    beta = jax.nn.sigmoid(pre[heads:])
    logdecay = -jnp.exp(decay_log)[:, None] * jax.nn.softplus(pre[:heads] + dt_bias[:, None])
    parts = logdecay.reshape(heads, -1, CHUNK)
    position = jnp.arange(CHUNK)
    upper = (position[:, None] <= position[None, :]).astype(F32)
    cumulative = jnp.einsum("hct,ts->hcs", parts, upper, precision=lax.Precision.HIGHEST)
    return cumulative.reshape(heads, -1), beta


def on_device(
    tokens_in,
    w_query,
    w_key,
    w_value,
    w_zgate,
    w_gates,
    w_out,
    decay_log,
    dt_bias,
    norm_gain,
    init_state,
    doc_trans,
    doc_state,
    retrieval,
    doc_place,
    assignment,
):
    heads = decay_log.shape[0]
    store_count = lax.axis_size("store")
    copies = store_count // heads
    swap = [(0, 1), (1, 0)]
    docs = jnp.concatenate([doc_trans, doc_state], axis=2)
    if copies > 1:
        docs = jnp.repeat(docs, copies, axis=1)
    docs = lax.all_to_all(docs, "store", split_axis=1, concat_axis=0, tiled=True)[:, 0]
    x = lax.all_gather(tokens_in, "head", axis=0, tiled=True)
    other_out = lax.ppermute(w_out, "head", swap)
    cumulative, beta = decays(x, w_gates, decay_log, dt_bias)
    gate, core, linear = delta_terms(x, w_query, w_key, w_value, w_zgate, cumulative, beta)
    order = doc_place[retrieval[assignment]]
    my_head = lax.axis_index("store") // copies
    init = lax.dynamic_index_in_dim(init_state, my_head, 0, keepdims=False)
    states = compose(order, init, docs)
    start = lax.all_to_all(states, "store", split_axis=0, concat_axis=0, tiled=True)[::copies]
    half = lax.axis_index("head").astype(jnp.int32).reshape(1)
    gain = norm_gain.reshape(1, DV)
    away = gated(1 - half, core, linear, gate, start, gain)
    received = lax.ppermute(away, "head", swap)
    own = gated(half, core, linear, gate, start, gain)
    return (mm(own, w_out) + mm(received, other_out)).astype(BF)


def solution(mesh):
    in_specs = (
        P(("groups", "store", "head"), None),
        P(None, "head"),
        P(None, "head"),
        P(None, "head"),
        P(None, "head"),
        P(None, None, "head"),
        P("head", None),
        P("head"),
        P("head"),
        P(),
        P("head", None, None),
        P(("groups", "store"), "head", None, None),
        P(("groups", "store"), "head", None, None),
        P("groups", None),
        P("groups"),
        P("groups"),
    )
    out_specs = P(("groups", "store", "head"), None)
    return jax.shard_map(
        on_device, mesh=mesh, in_specs=in_specs, out_specs=out_specs, check_vma=False
    )
```

```python
import jax
import jax.numpy as jnp
from jax import lax
from jax.experimental import pallas as pl
from jax.experimental.pallas import tpu as pltpu
from jax.sharding import PartitionSpec as P

DK = 128
DV = 128
CHUNK = 128
ROWS = 256
BF = jnp.bfloat16
F32 = jnp.float32


def mm(left, right):
    return jnp.dot(left, right, preferred_element_type=F32)


def unit_lower_inverses(mixes):
    size = mixes[0].shape[0]
    row = lax.broadcasted_iota(jnp.int32, (size, size), 0)
    col = lax.broadcasted_iota(jnp.int32, (size, size), 1)
    eye = jnp.where(row == col, 1.0, 0.0)
    inside = row // 16 == col // 16
    powers = [jnp.where(inside, -mix, 0.0) for mix in mixes]
    inverses = [eye + power for power in powers]
    powers = [mm(power.astype(BF), power.astype(BF)) for power in powers]
    for last in (False, False, True):
        if last:
            products = [mm(x.astype(BF), p.astype(BF)) for x, p in zip(inverses, powers)]
            inverses = [x + y for x, y in zip(inverses, products)]
        else:
            products = [
                mm(jnp.concatenate([x.astype(BF), p.astype(BF)], axis=0), p.astype(BF))
                for x, p in zip(inverses, powers)
            ]
            inverses = [x + y[:size] for x, y in zip(inverses, products)]
            powers = [y[size:] for y in products]
    width = 16
    while width < size:
        between = (row // (2 * width) == col // (2 * width)) & (row // width != col // width)
        narrow = [x.astype(BF) for x in inverses]
        steps = [mm(jnp.where(between, mix, 0.0).astype(BF), x) for mix, x in zip(mixes, narrow)]
        steps = [mm(x, step.astype(BF)) for x, step in zip(narrow, steps)]
        inverses = [x - step for x, step in zip(inverses, steps)]
        width *= 2
    return inverses


def terms_kernel(half, x, other, w_q, w_k, w_v, w_z, cols, rows, gate, qw, at_out, u_out, w_s, q_s, k_s, v_s):
    held = x.shape[0]
    chunks = 2 * held // CHUNK
    w_s[:, :DK] = w_q[...]
    w_s[:, DK:] = w_k[...]

    @pl.loop(0, held // ROWS)
    def project(tile):
        source = pl.ds(pl.multiple_of(tile * ROWS, ROWS), ROWS)
        for tokens, place in ((x, half[0]), (other, 1 - half[0])):
            at = pl.ds(pl.multiple_of(place * held + tile * ROWS, ROWS), ROWS)
            part = tokens[source, :]
            both = mm(part, w_s[...]).astype(BF).astype(F32)
            q, k = both[:, :DK], both[:, DK:]
            q_s[at, :] = (
                q * lax.rsqrt(jnp.sum(q * q, axis=-1, keepdims=True) + 1e-06) * DK ** (-0.5)
            ).astype(BF)
            k_s[at, :] = (k * lax.rsqrt(jnp.sum(k * k, axis=-1, keepdims=True) + 1e-06)).astype(BF)
            v_s[at, :] = mm(part, w_v[...]).astype(BF)
            gate[at, :] = mm(part, w_z[...]).astype(BF)

    group = min(4, chunks)

    @pl.loop(0, chunks // group)
    def terms(quarter):
        row = lax.broadcasted_iota(jnp.int32, (CHUNK, CHUNK), 0)
        col = lax.broadcasted_iota(jnp.int32, (CHUNK, CHUNK), 1)
        kept, mixes = [], []
        for inner in range(group):
            chunk = quarter * group + inner
            at = pl.ds(pl.multiple_of(chunk * CHUNK, CHUNK), CHUNK)
            q, k, v = q_s[at, :], k_s[at, :], v_s[at, :]
            both = lax.dot_general(
                jnp.concatenate([k, q], axis=0), k, (((1,), (1,)), ((), ())), preferred_element_type=F32
            )
            k_wide = k.astype(F32)
            k_turned = k_wide.T
            for e in range(2):
                cum_c = cols[0, at, e : e + 1]
                cum_r = rows[0, e : e + 1, at]
                beta_r = rows[0, 2 + e : 3 + e, at]
                decay = jnp.exp(jnp.where(row >= col, cum_c - cum_r, 0.0)) * beta_r
                mixes.append(jnp.where(row > col, decay * both[:CHUNK], 0.0))
                attend = jnp.where(row >= col, decay * both[CHUNK:], 0.0)
                growth = jnp.exp(cum_c)
                tail = jnp.exp(cum_r[:, CHUNK - 1 :] - cum_r) * beta_r
                at_out[e, chunk] = jnp.concatenate([attend, k_turned * tail], axis=0).astype(BF)
                qw[e, chunk, :CHUNK, :] = (growth * q.astype(F32)).astype(BF)
                side = jnp.concatenate(
                    [v[:, e * DV : (e + 1) * DV], (growth * k_wide).astype(BF)], axis=1
                )
                kept.append((e, chunk, side))
        for inverse, (e, chunk, side) in zip(unit_lower_inverses(mixes), kept):
            solved = mm(inverse.astype(BF), side)
            u_out[e, chunk] = solved[:, :DV]
            qw[e, chunk, CHUNK:, :] = solved[:, DV:].astype(BF)


def chunk_terms(half, x, other, w_query, w_key, w_value, w_zgate, cumulative, beta):
    held, width = x.shape
    tokens = 2 * held
    heads = beta.shape[0]
    steps = heads // 2
    chunks = tokens // CHUNK
    rows = jnp.concatenate([cumulative.reshape(steps, 2, tokens), beta.reshape(steps, 2, tokens)], axis=1)
    cols = jnp.swapaxes(rows, 1, 2)
    flops = 2 * tokens * width * 6 * DK * steps + heads * chunks * 26 * 2 * 128**3
    return pl.pallas_call(
        terms_kernel,
        grid=(steps,),
        in_specs=[
            pl.BlockSpec(memory_space=pltpu.SMEM),
            pl.BlockSpec((held, width), lambda i: (0, 0)),
            pl.BlockSpec((held, width), lambda i: (0, 0)),
            pl.BlockSpec((width, DK), lambda i: (0, i)),
            pl.BlockSpec((width, DK), lambda i: (0, i)),
            pl.BlockSpec((width, 2 * DV), lambda i: (0, i)),
            pl.BlockSpec((width, 2 * DV), lambda i: (0, i)),
            pl.BlockSpec((1, tokens, 4), lambda i: (i, 0, 0)),
            pl.BlockSpec((1, 4, tokens), lambda i: (i, 0, 0)),
        ],
        out_specs=[
            pl.BlockSpec((tokens, 2 * DV), lambda i: (0, i)),
            pl.BlockSpec((2, chunks, 2 * CHUNK, DK), lambda i: (i, 0, 0, 0)),
            pl.BlockSpec((2, chunks, CHUNK + DK, CHUNK), lambda i: (i, 0, 0, 0)),
            pl.BlockSpec((2, chunks, CHUNK, DV), lambda i: (i, 0, 0, 0)),
        ],
        out_shape=[
            jax.ShapeDtypeStruct((tokens, heads * DV), BF),
            jax.ShapeDtypeStruct((heads, chunks, 2 * CHUNK, DK), BF),
            jax.ShapeDtypeStruct((heads, chunks, CHUNK + DK, CHUNK), BF),
            jax.ShapeDtypeStruct((heads, chunks, CHUNK, DV), F32),
        ],
        scratch_shapes=[
            pltpu.VMEM((width, 2 * DK), BF),
            pltpu.VMEM((tokens, DK), BF),
            pltpu.VMEM((tokens, DK), BF),
            pltpu.VMEM((tokens, 2 * DV), BF),
        ],
        compiler_params=pltpu.CompilerParams(
            dimension_semantics=("arbitrary",), vmem_limit_bytes=56 * 2**20
        ),
        cost_estimate=pl.CostEstimate(flops=flops * 3, bytes_accessed=28 * 2**20, transcendentals=0),
    )(half, x, other, w_query, w_key, w_value, w_zgate, cols, rows)


def scan_kernel(closing, qw, at_in, u_in, core, linear, state):
    heads = qw.shape[0]
    chunk = pl.program_id(0)

    @pl.when(chunk == 0)
    def begin():
        row = lax.broadcasted_iota(jnp.int32, (DK, DV + DK), 0)
        col = lax.broadcasted_iota(jnp.int32, (DK, DV + DK), 1)
        start = jnp.where(row + DV == col, 1.0, 0.0)
        for head in range(heads):
            state[head] = start

    firsts = [mm(qw[head, 0], state[head].astype(BF)) for head in range(heads)]
    seconds = []
    for head, first in enumerate(firsts):
        lower = first[CHUNK:]
        u = jnp.concatenate([u_in[head, 0] - lower[:, :DV], -lower[:, DV:]], axis=1)
        seconds.append(mm(at_in[head, 0], u.astype(BF)))
    for head, (first, second) in enumerate(zip(firsts, seconds)):
        out = first[:CHUNK] + second[:CHUNK]
        core[:, head * DV : (head + 1) * DV] = out[:, :DV]
        linear[:, head * DK : (head + 1) * DK] = out[:, DV:].astype(BF)
        state[head] = closing[head, chunk] * state[head] + second[CHUNK:]


def scan_chunks(closing, qw, attend, u):
    heads, chunks = closing.shape
    tokens = chunks * CHUNK
    return pl.pallas_call(
        scan_kernel,
        grid=(chunks,),
        in_specs=[
            pl.BlockSpec(memory_space=pltpu.SMEM),
            pl.BlockSpec((heads, 1, 2 * CHUNK, DK), lambda c: (0, c, 0, 0)),
            pl.BlockSpec((heads, 1, CHUNK + DK, CHUNK), lambda c: (0, c, 0, 0)),
            pl.BlockSpec((heads, 1, CHUNK, DV), lambda c: (0, c, 0, 0)),
        ],
        out_specs=[
            pl.BlockSpec((CHUNK, heads * DV), lambda c: (c, 0)),
            pl.BlockSpec((CHUNK, heads * DK), lambda c: (c, 0)),
        ],
        out_shape=[
            jax.ShapeDtypeStruct((tokens, heads * DV), F32),
            jax.ShapeDtypeStruct((tokens, heads * DK), BF),
        ],
        scratch_shapes=[pltpu.VMEM((heads, DK, DV + DK), F32)],
        compiler_params=pltpu.CompilerParams(
            dimension_semantics=("arbitrary",), vmem_limit_bytes=56 * 2**20
        ),
        cost_estimate=pl.CostEstimate(
            flops=heads * chunks * 32 * 128**3, bytes_accessed=18 * 2**20, transcendentals=0
        ),
    )(closing, qw, attend, u)


def compose_kernel(order, init, docs, out):
    slots, listed = order.shape

    def advance(j, carry):
        for slot in range(slots):
            doc = order[slot, j]
            state = out[slot]
            high = state.astype(BF)
            low = (state - high.astype(F32)).astype(BF)
            moved = mm(docs[doc, :DK, :], jnp.concatenate([high, low], axis=1))
            out[slot] = moved[:, :DV] + moved[:, DV:] + docs[doc, DK:, :].astype(F32)
        return carry

    for slot in range(slots):
        out[slot] = init[...]
    lax.fori_loop(0, listed, advance, 0)


def compose(order, init, docs):
    slots, listed = order.shape
    return pl.pallas_call(
        compose_kernel,
        in_specs=[
            pl.BlockSpec(memory_space=pltpu.SMEM),
            pl.BlockSpec(memory_space=pltpu.VMEM),
            pl.BlockSpec(memory_space=pltpu.VMEM),
        ],
        out_specs=pl.BlockSpec(memory_space=pltpu.VMEM),
        out_shape=jax.ShapeDtypeStruct((slots, DK, DV), F32),
        compiler_params=pltpu.CompilerParams(vmem_limit_bytes=24 * 2**20),
        cost_estimate=pl.CostEstimate(
            flops=slots * listed * 4 * 128**3 * 8, bytes_accessed=4 * 2**20, transcendentals=0
        ),
    )(order, init, docs)


def gate_kernel(half, core, linear, gate, start, gain, out):
    del half
    for head in range(start.shape[0]):
        at = slice(head * DV, (head + 1) * DV)
        state = start[head]
        high = state.astype(BF)
        low = (state - high.astype(F32)).astype(BF)
        moved = mm(linear[:, at], jnp.concatenate([high, low], axis=1))
        values = core[:, at] + moved[:, :DV] + moved[:, DV:]
        z = gate[:, at].astype(F32)
        mean = jnp.mean(values * values, axis=-1, keepdims=True)
        out[:, at] = (values * lax.rsqrt(mean + 1e-06) * gain[...] * (z * jax.nn.sigmoid(z))).astype(BF)


def gated(half, core, linear, gate, start, gain):
    tokens, width = core.shape
    tiles = tokens // 2 // ROWS
    block = pl.BlockSpec((ROWS, width), lambda i, half: (half[0] * tiles + i, 0))
    return pl.pallas_call(
        gate_kernel,
        grid_spec=pltpu.PrefetchScalarGridSpec(
            num_scalar_prefetch=1,
            grid=(tiles,),
            in_specs=[
                block,
                block,
                block,
                pl.BlockSpec(start.shape, lambda i, half: (0, 0, 0)),
                pl.BlockSpec((1, DV), lambda i, half: (0, 0)),
            ],
            out_specs=pl.BlockSpec((ROWS, width), lambda i, half: (i, 0)),
        ),
        out_shape=jax.ShapeDtypeStruct((tokens // 2, width), BF),
        compiler_params=pltpu.CompilerParams(
            dimension_semantics=("arbitrary",), vmem_limit_bytes=56 * 2**20
        ),
        cost_estimate=pl.CostEstimate(flops=2**30, bytes_accessed=5 * 2**20, transcendentals=0),
    )(half, core, linear, gate, start, gain)


def project_kernel(own, received, w_own, w_other, out):
    out[...] = (mm(own[...], w_own[...]) + mm(received[...], w_other[...])).astype(BF)


def project_out(own, received, w_own, w_other):
    tokens, depth = own.shape
    width = w_own.shape[1]
    tile = 256
    left = pl.BlockSpec((tokens, depth), lambda i: (0, 0))
    right = pl.BlockSpec((depth, tile), lambda i: (0, i))
    return pl.pallas_call(
        project_kernel,
        grid=(width // tile,),
        in_specs=[left, left, right, right],
        out_specs=pl.BlockSpec((tokens, tile), lambda i: (0, i)),
        out_shape=jax.ShapeDtypeStruct((tokens, width), BF),
        compiler_params=pltpu.CompilerParams(
            dimension_semantics=("arbitrary",), vmem_limit_bytes=56 * 2**20
        ),
        cost_estimate=pl.CostEstimate(
            flops=4 * tokens * depth * width, bytes_accessed=12 * 2**20, transcendentals=0
        ),
    )(own, received, w_own, w_other)


def decays(half, x, other, w_gates, decay_log, dt_bias):
    heads = decay_log.shape[0]
    weights = jnp.concatenate([w_gates[0], w_gates[1]], axis=1)
    mine, theirs = (
        lax.dot_general(weights, part, (((0,), (1,)), ((), ())), preferred_element_type=F32)
        for part in (x, other)
    )
    pre = jnp.where(
        half[0] == 0, jnp.concatenate([mine, theirs], axis=1), jnp.concatenate([theirs, mine], axis=1)
    )
    pre = pre.astype(BF).astype(F32)
    beta = jax.nn.sigmoid(pre[heads:])
    logdecay = -jnp.exp(decay_log)[:, None] * jax.nn.softplus(pre[:heads] + dt_bias[:, None])
    parts = logdecay.reshape(heads, -1, CHUNK)
    position = jnp.arange(CHUNK)
    upper = (position[:, None] <= position[None, :]).astype(F32)
    cumulative = jnp.einsum("hct,ts->hcs", parts, upper, precision=lax.Precision.HIGHEST)
    return cumulative.reshape(heads, -1), beta


def on_device(
    tokens_in,
    w_query,
    w_key,
    w_value,
    w_zgate,
    w_gates,
    w_out,
    decay_log,
    dt_bias,
    norm_gain,
    init_state,
    doc_trans,
    doc_state,
    retrieval,
    doc_place,
    assignment,
):
    heads = decay_log.shape[0]
    store_count = lax.axis_size("store")
    copies = store_count // heads
    swap = [(0, 1), (1, 0)]
    docs = jnp.concatenate([doc_trans, doc_state], axis=2)
    if copies > 1:
        docs = jnp.repeat(docs, copies, axis=1)
    docs = lax.all_to_all(docs, "store", split_axis=1, concat_axis=0, tiled=True)[:, 0]
    other = lax.ppermute(tokens_in, "head", swap)
    other_out = lax.ppermute(w_out, "head", swap)
    half = lax.axis_index("head").astype(jnp.int32).reshape(1)
    cumulative, beta = decays(half, tokens_in, other, w_gates, decay_log, dt_bias)
    closing = jnp.exp(cumulative[:, CHUNK - 1 :: CHUNK])
    gate, qw, attend, u = chunk_terms(
        half, tokens_in, other, w_query, w_key, w_value, w_zgate, cumulative, beta
    )
    order = doc_place[retrieval[assignment]]
    my_head = lax.axis_index("store") // copies
    init = lax.dynamic_index_in_dim(init_state, my_head, 0, keepdims=False)
    init, order, closing, u = lax.optimization_barrier((init, order, closing, u))
    states = compose(order, init, docs)
    states, closing = lax.optimization_barrier((states, closing))
    start = lax.all_to_all(states, "store", split_axis=0, concat_axis=0, tiled=True)[::copies]
    core, linear = scan_chunks(closing, qw, attend, u)
    gain = norm_gain.reshape(1, DV)
    away = gated(1 - half, core, linear, gate, start, gain)
    received = lax.ppermute(away, "head", swap)
    own = gated(half, core, linear, gate, start, gain)
    return project_out(own, received, w_out, other_out)


def solution(mesh):
    in_specs = (
        P(("groups", "store", "head"), None),
        P(None, "head"),
        P(None, "head"),
        P(None, "head"),
        P(None, "head"),
        P(None, None, "head"),
        P("head", None),
        P("head"),
        P("head"),
        P(),
        P("head", None, None),
        P(("groups", "store"), "head", None, None),
        P(("groups", "store"), "head", None, None),
        P("groups", None),
        P("groups"),
        P("groups"),
    )
    out_specs = P(("groups", "store", "head"), None)
    return jax.shard_map(
        on_device, mesh=mesh, in_specs=in_specs, out_specs=out_specs, check_vma=False
    )
```

```python
import jax
import jax.numpy as jnp
from jax import lax
from jax.experimental import pallas as pl
from jax.experimental.pallas import tpu as pltpu
from jax.sharding import PartitionSpec as P

DK = 128
DV = 128
CHUNK = 128
ROWS = 256
GATE_ROWS = 256
OUT_COLUMNS = 512
BF = jnp.bfloat16
F32 = jnp.float32


def mm(left, right):
    return jnp.dot(left, right, preferred_element_type=F32)


def unit_lower_inverses(mixes):
    size = mixes[0].shape[0]
    row = lax.broadcasted_iota(jnp.int32, (size, size), 0)
    col = lax.broadcasted_iota(jnp.int32, (size, size), 1)
    eye = jnp.where(row == col, 1.0, 0.0)
    inside = row // 16 == col // 16
    powers = [jnp.where(inside, -mix, 0.0) for mix in mixes]
    inverses = [eye + power for power in powers]
    powers = [mm(power.astype(BF), power.astype(BF)) for power in powers]
    for last in (False, False, True):
        if last:
            products = [mm(x.astype(BF), p.astype(BF)) for x, p in zip(inverses, powers)]
            inverses = [x + y for x, y in zip(inverses, products)]
        else:
            products = [
                mm(jnp.concatenate([x.astype(BF), p.astype(BF)], axis=0), p.astype(BF))
                for x, p in zip(inverses, powers)
            ]
            inverses = [x + y[:size] for x, y in zip(inverses, products)]
            powers = [y[size:] for y in products]
    width = 16
    while width < size:
        between = (row // (2 * width) == col // (2 * width)) & (row // width != col // width)
        narrow = [x.astype(BF) for x in inverses]
        steps = [mm(jnp.where(between, mix, 0.0).astype(BF), x) for mix, x in zip(mixes, narrow)]
        steps = [mm(x, step.astype(BF)) for x, step in zip(narrow, steps)]
        inverses = [x - step for x, step in zip(inverses, steps)]
        width *= 2
    return inverses


def terms_kernel(half, x, other, w_q, w_k, w_v, w_z, cols, rows, gate, qw, at_out, u_out, w_s, q_s, k_s, v_s):
    held = x.shape[0]
    chunks = 2 * held // CHUNK
    w_s[:, :DK] = w_q[...]
    w_s[:, DK:] = w_k[...]

    @pl.loop(0, held // ROWS)
    def project(tile):
        source = pl.ds(pl.multiple_of(tile * ROWS, ROWS), ROWS)
        for tokens, place in ((x, half[0]), (other, 1 - half[0])):
            at = pl.ds(pl.multiple_of(place * held + tile * ROWS, ROWS), ROWS)
            part = tokens[source, :]
            both = mm(part, w_s[...]).astype(BF).astype(F32)
            q, k = both[:, :DK], both[:, DK:]
            q_s[at, :] = (
                q * lax.rsqrt(jnp.sum(q * q, axis=-1, keepdims=True) + 1e-06) * DK ** (-0.5)
            ).astype(BF)
            k_s[at, :] = (k * lax.rsqrt(jnp.sum(k * k, axis=-1, keepdims=True) + 1e-06)).astype(BF)
            v_s[at, :] = mm(part, w_v[...]).astype(BF)
            gate[at, :] = mm(part, w_z[...]).astype(BF)

    group = min(4, chunks)

    @pl.loop(0, chunks // group)
    def terms(quarter):
        row = lax.broadcasted_iota(jnp.int32, (CHUNK, CHUNK), 0)
        col = lax.broadcasted_iota(jnp.int32, (CHUNK, CHUNK), 1)
        kept, mixes = [], []
        for inner in range(group):
            chunk = quarter * group + inner
            at = pl.ds(pl.multiple_of(chunk * CHUNK, CHUNK), CHUNK)
            q, k, v = q_s[at, :], k_s[at, :], v_s[at, :]
            both = lax.dot_general(
                jnp.concatenate([k, q], axis=0), k, (((1,), (1,)), ((), ())), preferred_element_type=F32
            )
            k_wide = k.astype(F32)
            k_turned = k_wide.T
            for e in range(2):
                cum_c = cols[0, at, e : e + 1]
                cum_r = rows[0, e : e + 1, at]
                beta_r = rows[0, 2 + e : 3 + e, at]
                decay = jnp.exp(jnp.where(row >= col, cum_c - cum_r, 0.0)) * beta_r
                mixes.append(jnp.where(row > col, decay * both[:CHUNK], 0.0))
                attend = jnp.where(row >= col, decay * both[CHUNK:], 0.0)
                growth = jnp.exp(cum_c)
                tail = jnp.exp(cum_r[:, CHUNK - 1 :] - cum_r) * beta_r
                at_out[e, chunk] = jnp.concatenate([attend, k_turned * tail], axis=0).astype(BF)
                qw[e, chunk, :CHUNK, :] = (growth * q.astype(F32)).astype(BF)
                side = jnp.concatenate(
                    [v[:, e * DV : (e + 1) * DV], (growth * k_wide).astype(BF)], axis=1
                )
                kept.append((e, chunk, side))
        for inverse, (e, chunk, side) in zip(unit_lower_inverses(mixes), kept):
            solved = mm(inverse.astype(BF), side)
            u_out[e, chunk] = solved[:, :DV]
            qw[e, chunk, CHUNK:, :] = solved[:, DV:].astype(BF)


def chunk_terms(half, x, other, w_query, w_key, w_value, w_zgate, cumulative, beta):
    held, width = x.shape
    tokens = 2 * held
    heads = beta.shape[0]
    steps = heads // 2
    chunks = tokens // CHUNK
    rows = jnp.concatenate([cumulative.reshape(steps, 2, tokens), beta.reshape(steps, 2, tokens)], axis=1)
    cols = jnp.swapaxes(rows, 1, 2)
    flops = 2 * tokens * width * 6 * DK * steps + heads * chunks * 26 * 2 * 128**3
    return pl.pallas_call(
        terms_kernel,
        grid=(steps,),
        in_specs=[
            pl.BlockSpec(memory_space=pltpu.SMEM),
            pl.BlockSpec((held, width), lambda i: (0, 0)),
            pl.BlockSpec((held, width), lambda i: (0, 0)),
            pl.BlockSpec((width, DK), lambda i: (0, i)),
            pl.BlockSpec((width, DK), lambda i: (0, i)),
            pl.BlockSpec((width, 2 * DV), lambda i: (0, i)),
            pl.BlockSpec((width, 2 * DV), lambda i: (0, i)),
            pl.BlockSpec((1, tokens, 4), lambda i: (i, 0, 0)),
            pl.BlockSpec((1, 4, tokens), lambda i: (i, 0, 0)),
        ],
        out_specs=[
            pl.BlockSpec((tokens, 2 * DV), lambda i: (0, i)),
            pl.BlockSpec((2, chunks, 2 * CHUNK, DK), lambda i: (i, 0, 0, 0)),
            pl.BlockSpec((2, chunks, CHUNK + DK, CHUNK), lambda i: (i, 0, 0, 0)),
            pl.BlockSpec((2, chunks, CHUNK, DV), lambda i: (i, 0, 0, 0)),
        ],
        out_shape=[
            jax.ShapeDtypeStruct((tokens, heads * DV), BF),
            jax.ShapeDtypeStruct((heads, chunks, 2 * CHUNK, DK), BF),
            jax.ShapeDtypeStruct((heads, chunks, CHUNK + DK, CHUNK), BF),
            jax.ShapeDtypeStruct((heads, chunks, CHUNK, DV), F32),
        ],
        scratch_shapes=[
            pltpu.VMEM((width, 2 * DK), BF),
            pltpu.VMEM((tokens, DK), BF),
            pltpu.VMEM((tokens, DK), BF),
            pltpu.VMEM((tokens, 2 * DV), BF),
        ],
        compiler_params=pltpu.CompilerParams(
            dimension_semantics=("arbitrary",), vmem_limit_bytes=56 * 2**20
        ),
        cost_estimate=pl.CostEstimate(flops=flops * 3, bytes_accessed=28 * 2**20, transcendentals=0),
    )(half, x, other, w_query, w_key, w_value, w_zgate, cols, rows)


def scan_kernel(closing, qw, at_in, u_in, core, linear, state):
    heads = qw.shape[0]
    chunk = pl.program_id(0)

    @pl.when(chunk == 0)
    def begin():
        row = lax.broadcasted_iota(jnp.int32, (DK, DV + DK), 0)
        col = lax.broadcasted_iota(jnp.int32, (DK, DV + DK), 1)
        start = jnp.where(row + DV == col, 1.0, 0.0)
        for head in range(heads):
            state[head] = start

    firsts = [mm(qw[head, 0], state[head].astype(BF)) for head in range(heads)]
    seconds = []
    for head, first in enumerate(firsts):
        lower = first[CHUNK:]
        u = jnp.concatenate([u_in[head, 0] - lower[:, :DV], -lower[:, DV:]], axis=1)
        seconds.append(mm(at_in[head, 0], u.astype(BF)))
    for head, (first, second) in enumerate(zip(firsts, seconds)):
        out = first[:CHUNK] + second[:CHUNK]
        core[:, head * DV : (head + 1) * DV] = out[:, :DV]
        linear[:, head * DK : (head + 1) * DK] = out[:, DV:].astype(BF)
        state[head] = closing[head, chunk] * state[head] + second[CHUNK:]


def scan_chunks(closing, qw, attend, u):
    heads, chunks = closing.shape
    tokens = chunks * CHUNK
    return pl.pallas_call(
        scan_kernel,
        grid=(chunks,),
        in_specs=[
            pl.BlockSpec(memory_space=pltpu.SMEM),
            pl.BlockSpec((heads, 1, 2 * CHUNK, DK), lambda c: (0, c, 0, 0)),
            pl.BlockSpec((heads, 1, CHUNK + DK, CHUNK), lambda c: (0, c, 0, 0)),
            pl.BlockSpec((heads, 1, CHUNK, DV), lambda c: (0, c, 0, 0)),
        ],
        out_specs=[
            pl.BlockSpec((CHUNK, heads * DV), lambda c: (c, 0)),
            pl.BlockSpec((CHUNK, heads * DK), lambda c: (c, 0)),
        ],
        out_shape=[
            jax.ShapeDtypeStruct((tokens, heads * DV), F32),
            jax.ShapeDtypeStruct((tokens, heads * DK), BF),
        ],
        scratch_shapes=[pltpu.VMEM((heads, DK, DV + DK), F32)],
        compiler_params=pltpu.CompilerParams(
            dimension_semantics=("arbitrary",), vmem_limit_bytes=56 * 2**20
        ),
        cost_estimate=pl.CostEstimate(
            flops=heads * chunks * 32 * 128**3, bytes_accessed=18 * 2**20, transcendentals=0
        ),
    )(closing, qw, attend, u)


def compose_kernel(order, init, docs, out):
    slots, listed = order.shape

    def advance(j, carry):
        for slot in range(slots):
            doc = order[slot, j]
            state = out[slot]
            high = state.astype(BF)
            low = (state - high.astype(F32)).astype(BF)
            moved = mm(docs[doc, :DK, :], jnp.concatenate([high, low], axis=1))
            out[slot] = moved[:, :DV] + moved[:, DV:] + docs[doc, DK:, :].astype(F32)
        return carry

    for slot in range(slots):
        out[slot] = init[...]
    lax.fori_loop(0, listed, advance, 0)


def compose(order, init, docs):
    slots, listed = order.shape
    return pl.pallas_call(
        compose_kernel,
        in_specs=[
            pl.BlockSpec(memory_space=pltpu.SMEM),
            pl.BlockSpec(memory_space=pltpu.VMEM),
            pl.BlockSpec(memory_space=pltpu.VMEM),
        ],
        out_specs=pl.BlockSpec(memory_space=pltpu.VMEM),
        out_shape=jax.ShapeDtypeStruct((slots, DK, DV), F32),
        compiler_params=pltpu.CompilerParams(vmem_limit_bytes=24 * 2**20),
        cost_estimate=pl.CostEstimate(
            flops=slots * listed * 4 * 128**3 * 8, bytes_accessed=4 * 2**20, transcendentals=0
        ),
    )(order, init, docs)


def gate_kernel(half, core, linear, gate, start, gain, out):
    del half
    for head in range(start.shape[0]):
        at = slice(head * DV, (head + 1) * DV)
        values = core[:, at] + mm(linear[:, at], start[head])
        z = gate[:, at].astype(F32)
        mean = jnp.mean(values * values, axis=-1, keepdims=True)
        out[:, at] = (values * lax.rsqrt(mean + 1e-06) * gain[...] * (z * jax.nn.sigmoid(z))).astype(BF)


def gated(half, core, linear, gate, start, gain):
    tokens, width = core.shape
    tiles = tokens // 2 // GATE_ROWS
    block = pl.BlockSpec((GATE_ROWS, width), lambda i, half: (half[0] * tiles + i, 0))
    return pl.pallas_call(
        gate_kernel,
        grid_spec=pltpu.PrefetchScalarGridSpec(
            num_scalar_prefetch=1,
            grid=(tiles,),
            in_specs=[
                block,
                block,
                block,
                pl.BlockSpec(start.shape, lambda i, half: (0, 0, 0)),
                pl.BlockSpec((1, DV), lambda i, half: (0, 0)),
            ],
            out_specs=pl.BlockSpec((GATE_ROWS, width), lambda i, half: (i, 0)),
        ),
        out_shape=jax.ShapeDtypeStruct((tokens // 2, width), BF),
        compiler_params=pltpu.CompilerParams(
            dimension_semantics=("arbitrary",), vmem_limit_bytes=56 * 2**20
        ),
        cost_estimate=pl.CostEstimate(flops=2**30, bytes_accessed=5 * 2**20, transcendentals=0),
    )(half, core, linear, gate, start, gain)


def project_kernel(own, received, w_own, w_other, out):
    out[...] = (mm(own[...], w_own[...]) + mm(received[...], w_other[...])).astype(BF)


def project_out(own, received, w_own, w_other):
    tokens, depth = own.shape
    width = w_own.shape[1]
    tile = OUT_COLUMNS
    left = pl.BlockSpec((tokens, depth), lambda i: (0, 0))
    right = pl.BlockSpec((depth, tile), lambda i: (0, i))
    return pl.pallas_call(
        project_kernel,
        grid=(width // tile,),
        in_specs=[left, left, right, right],
        out_specs=pl.BlockSpec((tokens, tile), lambda i: (0, i)),
        out_shape=jax.ShapeDtypeStruct((tokens, width), BF),
        compiler_params=pltpu.CompilerParams(
            dimension_semantics=("arbitrary",), vmem_limit_bytes=56 * 2**20
        ),
        cost_estimate=pl.CostEstimate(
            flops=4 * tokens * depth * width, bytes_accessed=12 * 2**20, transcendentals=0
        ),
    )(own, received, w_own, w_other)


def decays(half, x, other, w_gates, decay_log, dt_bias):
    heads = decay_log.shape[0]
    weights = jnp.concatenate([w_gates[0], w_gates[1]], axis=1)
    mine, theirs = (
        lax.dot_general(weights, part, (((0,), (1,)), ((), ())), preferred_element_type=F32)
        for part in (x, other)
    )
    pre = jnp.where(
        half[0] == 0, jnp.concatenate([mine, theirs], axis=1), jnp.concatenate([theirs, mine], axis=1)
    )
    pre = pre.astype(BF).astype(F32)
    beta = jax.nn.sigmoid(pre[heads:])
    logdecay = -jnp.exp(decay_log)[:, None] * jax.nn.softplus(pre[:heads] + dt_bias[:, None])
    parts = logdecay.reshape(heads, -1, CHUNK)
    position = jnp.arange(CHUNK)
    upper = (position[:, None] <= position[None, :]).astype(F32)
    cumulative = jnp.einsum("hct,ts->hcs", parts, upper, precision=lax.Precision.HIGHEST)
    return cumulative.reshape(heads, -1), beta


def on_device(
    tokens_in,
    w_query,
    w_key,
    w_value,
    w_zgate,
    w_gates,
    w_out,
    decay_log,
    dt_bias,
    norm_gain,
    init_state,
    doc_trans,
    doc_state,
    retrieval,
    doc_place,
    assignment,
):
    heads = decay_log.shape[0]
    store_count = lax.axis_size("store")
    copies = store_count // heads
    swap = [(0, 1), (1, 0)]
    docs = jnp.concatenate([doc_trans, doc_state], axis=2)
    if copies > 1:
        docs = jnp.repeat(docs, copies, axis=1)
    docs = lax.all_to_all(docs, "store", split_axis=1, concat_axis=0, tiled=True)[:, 0]
    other = lax.ppermute(tokens_in, "head", swap)
    other_out = lax.ppermute(w_out, "head", swap)
    half = lax.axis_index("head").astype(jnp.int32).reshape(1)
    cumulative, beta = decays(half, tokens_in, other, w_gates, decay_log, dt_bias)
    closing = jnp.exp(cumulative[:, CHUNK - 1 :: CHUNK])
    gate, qw, attend, u = chunk_terms(
        half, tokens_in, other, w_query, w_key, w_value, w_zgate, cumulative, beta
    )
    order = doc_place[retrieval[assignment]]
    my_head = lax.axis_index("store") // copies
    init = lax.dynamic_index_in_dim(init_state, my_head, 0, keepdims=False)
    init, order, closing, u = lax.optimization_barrier((init, order, closing, u))
    states = compose(order, init, docs)
    states, closing = lax.optimization_barrier((states, closing))
    start = lax.all_to_all(states.astype(BF), "store", split_axis=0, concat_axis=0, tiled=True)[::copies]
    core, linear = scan_chunks(closing, qw, attend, u)
    gain = norm_gain.reshape(1, DV)
    away = gated(1 - half, core, linear, gate, start, gain)
    received = lax.ppermute(away, "head", swap)
    own = gated(half, core, linear, gate, start, gain)
    return project_out(own, received, w_out, other_out)


def solution(mesh):
    in_specs = (
        P(("groups", "store", "head"), None),
        P(None, "head"),
        P(None, "head"),
        P(None, "head"),
        P(None, "head"),
        P(None, None, "head"),
        P("head", None),
        P("head"),
        P("head"),
        P(),
        P("head", None, None),
        P(("groups", "store"), "head", None, None),
        P(("groups", "store"), "head", None, None),
        P("groups", None),
        P("groups"),
        P("groups"),
    )
    out_specs = P(("groups", "store", "head"), None)
    return jax.shard_map(
        on_device, mesh=mesh, in_specs=in_specs, out_specs=out_specs, check_vma=False
    )
```
